512 devices in a mesh: seq: 64 (over x, z, core), tensor: 8 (over y).
Axes of the slice: x: 4, y: 8, z: 8, core: 2. Of those that a mesh axis runs over, the one named last changes fastest.
Arguments:
- queries: bfloat16 [8192, 12288], P(('seq', 'tensor')), may hold values from -5 to 5
- keys: bfloat16 [8192, 1024], P(('seq', 'tensor')), may hold values from -5 to 5
- values: bfloat16 [8192, 1024], P(('seq', 'tensor')), may hold values from -6 to 6
- tile_len: int32 [64], replicated, may hold values from 2 to 128, as said below
- ancestors: int32 [64, 52], P('seq'), may hold values from -1 to 62, as said below
Outputs:
- attended: bfloat16 [8192, 12288], P(('seq', 'tensor'))
The draws below stay inside these ranges and needn't reach their ends.
Inputs may be any that keep to these rules, and one draw needn't show every extreme that they name: `tile_len`: some tile is full. `ancestors`: the shards form a tree: shard 0 is the root; the list of shard s is its parent's list followed by the parent's first tile (tile number p, since 1 = 1), where the parent p is an earlier shard; entries are ordered from the root and padded at the end with -1; some shard lists exactly 52 tiles.
All inputs are finite; a program needn't handle non-finite values.
Results may differ from the reference program's by a relative error of at most 0.0065.
Values may be sent and summed in bfloat16 or wider, within the bound.
No kernel may reach another device: no remote copies, remote signals or barrier semaphores. Data moves between devices by JAX's collectives and lax.ppermute only.
A program may use at most 64 MiB of HBM per device.

```python
import math
import jax
import jax.numpy as jnp
from jax import lax

HEADS = 96
KV = 8
HD = 128
TILE = 128
TILE_DEV = 1
ANC = 52
TILES = 64
TOKENS = 8192
N_SEQ = 64


def draw_queries(key, part):
    key = jax.random.fold_in(key, 12)
    base = jnp.clip(1.5 * jax.random.normal(key, (TOKENS, HEADS * HD), jnp.float32), -5.0, 5.0)
    return base.astype(jnp.bfloat16)


def draw_keys(key, part):
    key = jax.random.fold_in(key, 11)
    base = jnp.clip(1.5 * jax.random.normal(key, (TOKENS, KV * HD), jnp.float32), -5.0, 5.0)
    return base.astype(jnp.bfloat16)


def draw_tile_len(key, part):
    key = jax.random.fold_in(key, 3)
    len_key, spot_key = jax.random.split(key)
    lengths = jax.random.randint(len_key, (TILES,), 2, TILE + 1)
    spot = jax.random.randint(spot_key, (), 0, TILES)
    return jnp.where(jnp.arange(TILES, dtype=jnp.int32) == spot, TILE, lengths).astype(jnp.int32)


def draw_ancestors(key, part):
    key = jax.random.fold_in(key, 5)
    chain_key, pick_key = jax.random.split(key)
    order = jax.random.permutation(chain_key, N_SEQ - 1) + 1
    member = jnp.zeros((N_SEQ,), jnp.int32).at[order[:ANC]].set(1)
    jitter = jax.random.randint(pick_key, (N_SEQ, N_SEQ), 0, 4)
    earlier = jnp.arange(N_SEQ, dtype=jnp.int32)
    slot_ids = jnp.arange(ANC, dtype=jnp.int32)

    def place_shard(carry, item):
        depths, lists, last_member = carry
        shard_id, is_member, noise_row = item
        eligible = (earlier < shard_id) & (depths < ANC)
        ranking = jnp.where(eligible, (depths + noise_row) * N_SEQ + earlier, -1)
        parent = jnp.where(is_member > 0, last_member, jnp.argmax(ranking).astype(jnp.int32))
        new_row = jnp.where(slot_ids == depths[parent], TILE_DEV * parent, lists[parent])
        lists = lists.at[shard_id].set(new_row)
        depths = depths.at[shard_id].set(depths[parent] + 1)
        last_member = jnp.where(is_member > 0, shard_id, last_member)
        return ((depths, lists, last_member), None)
    start_state = (jnp.zeros((N_SEQ,), jnp.int32), jnp.full((N_SEQ, ANC), -1, jnp.int32), jnp.int32(0))
    final_state, unused = lax.scan(place_shard, start_state, (earlier[1:], member[1:], jitter[1:]))
    return final_state[1]


def steps_of(own_key, dims, cuts, low, high):
    def one(dim, blocks):
        heights = jax.random.uniform(jax.random.fold_in(jax.random.fold_in(own_key, 6), dim), (blocks,), jnp.float32, low / len(cuts), high / len(cuts))
        return jnp.repeat(jnp.exp(heights), dims[dim] // blocks).reshape((-1,) + (1,) * (len(dims) - dim - 1))

    loudness = one(*cuts[0])
    for cut in cuts[1:]:
        loudness = loudness * one(*cut)
    return loudness


def bell_draw(key, shape, scale, bound, pieces=(), kind=jnp.bfloat16):
    gain = steps_of(key, shape, pieces, -0.22, 0.18) if pieces else 1.0
    drawn = jax.random.normal(key, shape, jnp.float32) * scale * gain
    return jnp.minimum(jnp.maximum(drawn, -bound), bound).astype(kind)


def setup_inputs(seed: int = 0) -> dict:
    key_of = jax.random.split(jax.random.key(seed), 6)
    queries = draw_queries(jax.random.fold_in(key_of[5], 71), 0)
    keys = draw_keys(jax.random.fold_in(key_of[5], 71), 0)
    values = bell_draw(key_of[2], (TOKENS, KV * HD), 1.0, 6.0, ((0, 512),))
    tile_len = draw_tile_len(jax.random.fold_in(key_of[5], 71), 0)
    ancestors = draw_ancestors(jax.random.fold_in(key_of[5], 71), 0)
    return {"queries": queries, "keys": keys, "values": values, "tile_len": tile_len, "ancestors": ancestors}


def reference(queries, keys, values, tile_len, ancestors):
    per_group = HEADS // KV
    tok_count = TILE * TILE_DEV
    scaling = 1.0 / math.sqrt(HD)
    query_all = queries.reshape(N_SEQ, tok_count, KV, per_group, HD)
    key_local = keys.reshape(N_SEQ, tok_count, KV, HD)
    val_local = values.reshape(N_SEQ, tok_count, KV, HD)
    key_tiles = keys.reshape(TILES, TILE, KV, HD)
    val_tiles = values.reshape(TILES, TILE, KV, HD)
    offsets = jnp.arange(TILE, dtype=jnp.int32)
    positions = jnp.arange(tok_count, dtype=jnp.int32)

    def one_shard(shard_id):
        query_block = query_all[shard_id].astype(jnp.float32)
        listed = ancestors[shard_id]
        live_slot = listed >= 0
        safe_ids = jnp.maximum(listed, 0).astype(jnp.int32)
        key_far = key_tiles[safe_ids].reshape(ANC * TILE, KV, HD)
        val_far = val_tiles[safe_ids].reshape(ANC * TILE, KV, HD)
        own_len = lax.dynamic_slice_in_dim(tile_len, (shard_id * TILE_DEV).astype(jnp.int32), TILE_DEV)
        own_valid = positions % TILE < jnp.repeat(own_len, TILE, total_repeat_length=tok_count)
        near_mask = own_valid[None, :] & (positions[None, :] <= positions[:, None])
        far_valid = (live_slot[:, None] & (offsets[None, :] < tile_len[safe_ids][:, None])).reshape(ANC * TILE)
        far_mask = jnp.broadcast_to(far_valid[None, :], (tok_count, ANC * TILE))
        visible = jnp.concatenate([near_mask, far_mask], axis=1)
        key_all = jnp.concatenate([key_local[shard_id], key_far], axis=0).astype(jnp.float32)
        val_all = jnp.concatenate([val_local[shard_id], val_far], axis=0).astype(jnp.float32)
        scores = jnp.einsum('iqrd,kqd->qrik', query_block, key_all) * scaling
        scores = jnp.where(visible, scores, -jnp.inf)
        row_max = lax.optimization_barrier(jnp.max(scores, axis=-1, keepdims=True))
        weights = jnp.where(visible, jnp.exp(scores - row_max), 0.0).astype(jnp.bfloat16)
        total = lax.optimization_barrier(jnp.sum(weights.astype(jnp.float32), axis=-1))
        summed = jnp.einsum('qrik,kqd->iqrd', weights.astype(jnp.float32), val_all)
        result = summed / jnp.moveaxis(total, 2, 0)[..., None]
        return result.astype(jnp.bfloat16).reshape(tok_count, HEADS * HD)
    stacked = lax.map(one_shard, jnp.arange(N_SEQ, dtype=jnp.int32))
    return stacked.reshape(TOKENS, HEADS * HD)
```

```python
import functools
import math

import jax
import jax.numpy as jnp
from jax import lax
from jax.experimental import pallas as pl
from jax.experimental.pallas import tpu as pltpu
from jax.sharding import Mesh, PartitionSpec as P

HEADS = 96
KV = 8
HD = 128
TILE = 128
GROUP = HEADS // KV
NX, NZ, NC, NT = 4, 8, 2, 8
BIG = -1e30
LOG2E = 1.4426950408889634
SCALE2 = LOG2E / math.sqrt(HD)
F32 = jnp.float32
BF16 = jnp.bfloat16


def attend(h, s, vext, m_ref, acc_ref):
    old = m_ref[h]
    top = jnp.max(s, axis=1, keepdims=True)
    new = jnp.maximum(old, top)
    p = jnp.exp2((s - new[:, :1]) * SCALE2).astype(BF16)
    keep = jnp.exp2((old - new) * SCALE2)
    part = jnp.dot(p, vext, preferred_element_type=F32)
    acc_ref[h] = acc_ref[h] * jnp.concatenate([keep, keep], axis=1) + part
    m_ref[h] = new


def query(q_ref, h):
    lane = lax.broadcasted_iota(jnp.int32, (TILE, TILE), 1)
    one = jnp.where(lane == 0, 1.0, 0.0).astype(BF16)
    return jnp.concatenate([q_ref[:, pl.ds(pl.multiple_of(h * HD, HD), HD)], one], axis=1)


def own_tile(own_len, q_ref, own_ref, m_ref, acc_ref):
    row = lax.broadcasted_iota(jnp.int32, (TILE, TILE), 0)
    col = lax.broadcasted_iota(jnp.int32, (TILE, TILE), 1)
    seen = (col <= row) & (col < own_len)
    key = own_ref[:, :HD]
    vext = jnp.concatenate([own_ref[:, HD:], jnp.ones((TILE, HD), BF16)], axis=1)

    def head(h, carry):
        q = q_ref[:, pl.ds(pl.multiple_of(h * HD, HD), HD)]
        s = lax.dot_general(q, key, (((1,), (1,)), ((), ())), preferred_element_type=F32)
        s = jnp.where(seen, s, BIG)
        top = jnp.max(s, axis=1, keepdims=True)
        p = jnp.exp2((s - top) * SCALE2).astype(BF16)
        acc_ref[h] = jnp.dot(p, vext, preferred_element_type=F32)
        m_ref[h] = jnp.broadcast_to(top, (TILE, HD))
        return carry

    lax.fori_loop(0, GROUP, head, 0)


def far_tiles(eff_ref, base, q_ref, kv_ref, key_t, vext, m_ref, acc_ref):
    tiles = kv_ref.shape[0]
    lane = lax.broadcasted_iota(jnp.int32, (TILE, TILE), 1)
    total = eff_ref[base]
    for i in range(1, tiles):
        total = total + eff_ref[base + i]

    @pl.when(total > 0)
    def _():
        for i in range(tiles):
            at = slice(i * TILE, (i + 1) * TILE)
            key_t[:HD, at] = kv_ref[i, :, :HD].T
            key_t[HD:, at] = jnp.where(lane < eff_ref[base + i], 0.0, BIG).astype(BF16)
            vext[at, :HD] = kv_ref[i, :, HD:]
            vext[at, HD:] = jnp.ones((TILE, HD), BF16)

        def head(h, carry):
            s = jnp.dot(query(q_ref, h), key_t[...], preferred_element_type=F32)
            attend(h, s, vext[...], m_ref, acc_ref)
            return carry

        lax.fori_loop(0, GROUP, head, 0)


def first_kernel(eff, q, own, a, b, m, acc, key_t, vext):
    own_tile(eff[0], q, own, m, acc)
    far_tiles(eff, 1, q, a, key_t, vext, m, acc)
    far_tiles(eff, 9, q, b, key_t, vext, m, acc)


def middle_kernel(eff, q, a, b, m_in, acc_in, m, acc, key_t, vext):
    m[...] = m_in[...]
    acc[...] = acc_in[...]
    far_tiles(eff, 0, q, a, key_t, vext, m, acc)
    far_tiles(eff, 8, q, b, key_t, vext, m, acc)


def last_kernel(eff, q, a, b, m_in, acc_in, out, m, acc, key_t, vext):
    m[...] = m_in[...]
    acc[...] = acc_in[...]
    far_tiles(eff, 0, q, a, key_t, vext, m, acc)
    far_tiles(eff, 8, q, b, key_t, vext, m, acc)

    def head(h, carry):
        val = acc[h]
        res = (val[:, :HD] / val[:, HD:]).astype(BF16)
        out[:, pl.ds(pl.multiple_of(h * HD, HD), HD)] = res
        return carry

    lax.fori_loop(0, GROUP, head, 0)


VM = pl.BlockSpec(memory_space=pltpu.VMEM)
SM = pl.BlockSpec(memory_space=pltpu.SMEM)
STATE = (
    jax.ShapeDtypeStruct((GROUP, TILE, HD), F32),
    jax.ShapeDtypeStruct((GROUP, TILE, 2 * HD), F32),
)
WORK = [pltpu.VMEM((2 * HD, NZ * TILE), BF16), pltpu.VMEM((NZ * TILE, 2 * HD), BF16)]
PARAMS = pltpu.CompilerParams(vmem_limit_bytes=24 * 1024 * 1024)


def cost(tiles):
    return pl.CostEstimate(
        flops=tiles * GROUP * TILE * TILE * 256 * 4,
        bytes_accessed=4 * 1024 * 1024,
        transcendentals=tiles * GROUP * TILE * TILE,
    )


def first(eff, q, own, a, b):
    return pl.pallas_call(
        first_kernel,
        out_shape=STATE,
        in_specs=[SM, VM, VM, VM, VM],
        out_specs=(VM, VM),
        scratch_shapes=WORK,
        compiler_params=PARAMS,
        cost_estimate=cost(17),
    )(eff, q, own, a, b)


def middle(eff, q, a, b, state):
    return pl.pallas_call(
        middle_kernel,
        out_shape=STATE,
        in_specs=[SM, VM, VM, VM, VM, VM],
        out_specs=(VM, VM),
        scratch_shapes=WORK,
        compiler_params=PARAMS,
        cost_estimate=cost(16),
    )(eff, q, a, b, *state)


def last(eff, q, a, b, state):
    return pl.pallas_call(
        last_kernel,
        out_shape=jax.ShapeDtypeStruct((TILE, GROUP * HD), BF16),
        in_specs=[SM, VM, VM, VM, VM, VM],
        out_specs=VM,
        scratch_shapes=[pltpu.VMEM(s.shape, s.dtype) for s in STATE] + WORK,
        compiler_params=PARAMS,
        cost_estimate=cost(16),
    )(eff, q, a, b, *state)


def flip(a):
    return lax.ppermute(a, "c", [(0, 1), (1, 0)])


def along(a):
    pairs = []
    for x in range(NX):
        for c in range(NC):
            to = (x + 1) % NX if c == 0 else (x - 1) % NX
            pairs.append((x * NC + c, to * NC + c))
    return lax.ppermute(a, ("x", "c"), pairs)


def local(queries, keys, values, tile_len, ancestors):
    rows = queries.shape[0]
    x, z, c = (lax.axis_index(n) for n in ("x", "z", "c"))

    kv = jnp.concatenate([keys.reshape(rows, KV, HD), values.reshape(rows, KV, HD)], axis=2)
    own = lax.all_to_all(kv.transpose(1, 0, 2), "t", 0, 0, tiled=True).reshape(TILE, 2 * HD)
    line = lax.all_to_all(jnp.broadcast_to(own, (NZ, TILE, 2 * HD)), "z", 0, 0, tiled=True)

    listed = ancestors[0]
    tiles = jnp.arange(tile_len.shape[0], dtype=jnp.int32)
    hit = jnp.any(listed[:, None] == tiles[None, :], axis=0)
    eff = jnp.where(hit, tile_len, 0).reshape(NX, NZ, NC)
    near = jnp.where(c == 0, (x + 3) % NX, (x + 1) % NX)
    other = jnp.where(c == 0, (x + 1) % NX, (x + 3) % NX)
    opposite = (x + 2) % NX

    def lens(xi, ci):
        return lax.dynamic_slice(eff, (xi, 0, ci), (1, NZ, 1)).reshape(NZ)

    own_len = lax.dynamic_slice(tile_len, ((x * NZ + z) * NC + c,), (1,))
    eff0 = jnp.concatenate([own_len, lens(x, c), lens(x, 1 - c)])
    eff1 = jnp.concatenate([lens(near, c), lens(other, 1 - c)])
    eff2 = jnp.concatenate([lens(near, 1 - c), lens(other, c)])
    eff3 = jnp.concatenate([lens(opposite, c), lens(opposite, 1 - c)])

    q = queries.reshape(rows, KV, GROUP * HD).transpose(1, 0, 2)
    q = lax.all_to_all(q, "t", 0, 0, tiled=True).reshape(TILE, GROUP * HD)

    p1 = along(line)
    c0 = flip(line)
    p2 = along(c0)
    state = first(eff0, q, own, line, c0)
    p3 = along(p1)
    c1 = flip(p1)
    state = middle(eff1, q, p1, c1, state)
    c2 = flip(p2)
    state = middle(eff2, q, p2, c2, state)
    c3 = flip(p3)
    out = last(eff3, q, p3, c3, state)

    out = lax.all_to_all(out.reshape(NT, rows, GROUP * HD), "t", 0, 0, tiled=True)
    return out.transpose(1, 0, 2).reshape(rows, HEADS * HD)


def solution(mesh):
    fine = Mesh(mesh.devices.reshape(NX, NZ, NC, NT), ("x", "z", "c", "t"))
    split = P(("x", "z", "c", "t"), None)
    in_specs = (split, split, split, P(), P(("x", "z", "c"), None))
    return jax.shard_map(local, mesh=fine, in_specs=in_specs, out_specs=split, check_vma=False)
```

```python
import functools
import math

import jax
import jax.numpy as jnp
from jax import lax
from jax.experimental import pallas as pl
from jax.experimental.pallas import tpu as pltpu
from jax.sharding import Mesh, PartitionSpec as P

HEADS = 96
KV = 8
HD = 128
TILE = 128
GROUP = HEADS // KV
NX, NZ, NC, NT = 4, 8, 2, 8
BIG = -1e30
STEP = 16
WIDE = 512
LOG2E = 1.4426950408889634
SCALE2 = LOG2E / math.sqrt(HD)
F32 = jnp.float32
BF16 = jnp.bfloat16


def soften(s, old):
    parts = [s[:, j : j + HD] for j in range(0, s.shape[1], HD)]
    top = functools.reduce(jnp.maximum, parts)
    new = jnp.maximum(old, jnp.max(top, axis=1, keepdims=True))
    p = jnp.concatenate([jnp.exp2((x - new) * SCALE2).astype(BF16) for x in parts], axis=1)
    return p, jnp.exp2((old - new) * SCALE2), new


def own_tile(own_len, q_ref, own_ref, m_ref, acc_ref):
    row = lax.broadcasted_iota(jnp.int32, (TILE, TILE), 0)
    col = lax.broadcasted_iota(jnp.int32, (TILE, TILE), 1)
    seen = (col <= row) & (col < own_len)
    key_t = own_ref[:, :HD].T
    vext = jnp.concatenate([own_ref[:, HD:], jnp.ones((TILE, HD), BF16)], axis=1)
    for h in range(GROUP):
        s = jnp.dot(q_ref[:, h * HD : (h + 1) * HD], key_t, preferred_element_type=F32)
        s = jnp.where(seen, s, BIG)
        top = jnp.broadcast_to(jnp.max(s, axis=1, keepdims=True), (TILE, HD))
        p = jnp.exp2((s - top) * SCALE2).astype(BF16)
        acc_ref[h] = jnp.dot(p, vext, preferred_element_type=F32)
        m_ref[h] = top


def far_tiles(eff_ref, base, q_ref, kv_refs, packed, bias, m_ref, acc_ref):
    row = lax.broadcasted_iota(jnp.int32, (TILE, HD), 0)
    lane = lax.broadcasted_iota(jnp.int32, (TILE, HD), 1)
    one = jnp.where(lane == 0, 1.0, 0.0).astype(BF16)
    count = jnp.int32(0)
    slot = base
    for kv_ref in kv_refs:
        for i in range(kv_ref.shape[0]):
            valid = eff_ref[slot]
            at = pl.ds(pl.multiple_of(count, STEP), TILE)
            packed[at, :] = kv_ref[i]
            bias[at, :] = jnp.where(row < valid, 0.0, BIG).astype(BF16)
            count = count + lax.div(valid + (STEP - 1), STEP) * STEP
            slot += 1
    at = pl.ds(pl.multiple_of(count, STEP), WIDE)
    packed[at, :] = jnp.zeros((WIDE, 2 * HD), BF16)
    bias[at, :] = jnp.full((WIDE, HD), BIG, BF16)

    def block(start, size):
        at = pl.ds(pl.multiple_of(start, WIDE // 2), size)
        key_t = jnp.concatenate([packed[at, :HD].T, bias[at, :].T], axis=0)
        vext = jnp.concatenate([packed[at, HD:], jnp.ones((size, HD), BF16)], axis=1)
        for h in range(GROUP):
            q = jnp.concatenate([q_ref[:, h * HD : (h + 1) * HD], one], axis=1)
            s = jnp.dot(q, key_t, preferred_element_type=F32)
            p, keep, m_ref[h] = soften(s, m_ref[h])
            part = jnp.dot(p, vext, preferred_element_type=F32)
            acc_ref[h] = acc_ref[h] * jnp.concatenate([keep, keep], axis=1) + part

    def step(k, carry):
        block(k * WIDE, WIDE)
        return carry

    wide = lax.div(count + (WIDE // 2 - 1), WIDE)
    lax.fori_loop(0, wide, step, 0)

    @pl.when(count > wide * WIDE)
    def _():
        block(wide * WIDE, WIDE // 2)


def first_kernel(base, eff, q, own, a, b, m, acc, packed, bias):
    own_tile(eff[64], q, own, m, acc)
    far_tiles(eff, base, q, (a, b), packed, bias, m, acc)


def middle_kernel(base, eff, q, a, b, m_in, acc_in, m, acc, packed, bias):
    m[...] = m_in[...]
    acc[...] = acc_in[...]
    far_tiles(eff, base, q, (a, b), packed, bias, m, acc)


def last_kernel(base, eff, q, a, b, m_in, acc_in, out, m, acc, packed, bias):
    m[...] = m_in[...]
    acc[...] = acc_in[...]
    far_tiles(eff, base, q, (a, b), packed, bias, m, acc)
    for h in range(GROUP):
        val = acc[h]
        out[:, h * HD : (h + 1) * HD] = (val[:, :HD] / val[:, HD:]).astype(BF16)


VM = pl.BlockSpec(memory_space=pltpu.VMEM)
SM = pl.BlockSpec(memory_space=pltpu.SMEM)
STATE = (
    jax.ShapeDtypeStruct((GROUP, TILE, HD), F32),
    jax.ShapeDtypeStruct((GROUP, TILE, 2 * HD), F32),
)
ROWS = 2 * NZ * TILE + WIDE
WORK = [pltpu.VMEM((ROWS, 2 * HD), BF16), pltpu.VMEM((ROWS, HD), BF16)]
PARAMS = pltpu.CompilerParams(vmem_limit_bytes=24 * 1024 * 1024)


def busy(us):
    return pl.CostEstimate(flops=int(us * 1e9), bytes_accessed=1024, transcendentals=1024)


LIGHT = pl.CostEstimate(flops=1, bytes_accessed=1, transcendentals=1)


def first(base, eff, q, own, a, b):
    return pl.pallas_call(
        functools.partial(first_kernel, base),
        out_shape=STATE,
        in_specs=[SM, VM, VM, VM, VM],
        out_specs=(VM, VM),
        scratch_shapes=WORK,
        compiler_params=PARAMS,
        cost_estimate=busy(6),
    )(eff, q, own, a, b)


def middle(base, eff, q, a, b, state):
    return pl.pallas_call(
        functools.partial(middle_kernel, base),
        out_shape=STATE,
        in_specs=[SM, VM, VM, VM, VM, VM],
        out_specs=(VM, VM),
        scratch_shapes=WORK,
        compiler_params=PARAMS,
        cost_estimate=busy(5),
    )(eff, q, a, b, *state)


def last(base, eff, q, a, b, state):
    return pl.pallas_call(
        functools.partial(last_kernel, base),
        out_shape=jax.ShapeDtypeStruct((TILE, GROUP * HD), BF16),
        in_specs=[SM, VM, VM, VM, VM, VM],
        out_specs=VM,
        scratch_shapes=[pltpu.VMEM(s.shape, s.dtype) for s in STATE] + WORK,
        compiler_params=PARAMS,
        cost_estimate=busy(4),
    )(eff, q, a, b, *state)


def flip(a):
    return lax.ppermute(a, "c", [(0, 1), (1, 0)])


def along(a, step, wanted):
    pairs = []
    for x in range(NX):
        for c in range(NC):
            to = (x + step) % NX if c == 0 else (x - step) % NX
            if (c, x, to) in wanted:
                pairs.append((x * NC + c, to * NC + c))
    return lax.ppermute(a, ("x", "c"), pairs)


def flip_from(a, low):
    pairs = [(x * NC + c, x * NC + 1 - c) for x in range(low, NX) for c in range(NC)]
    return lax.ppermute(a, ("x", "c"), pairs)


NEXT = {(c, x, x + 1) for c in range(NC) for x in range(NX - 1)} | {(c, 0, NX - 1) for c in range(NC)}
FIRST = NEXT | {(1, 1, 0)}
THIRD = {(0, 1, 2), (0, 2, 3), (1, 3, 2), (1, 0, 3)}


barrier = lax.optimization_barrier


def seen_lengths(tile_len, listed, x, z, c):
    i = jnp.arange(72, dtype=jnp.int32)
    buf, slot = i // 8, i % 8
    core = jnp.where(buf % 2 == 0, c, 1 - c)
    side = jnp.where(c == 0, -1, 1)
    dx = jnp.where((buf < 2) | (buf == 8), 0, jnp.where(buf >= 6, 2, jnp.where((buf == 2) | (buf == 5), side, -side)))
    zi = jnp.where(buf == 8, z, slot)
    ids = (((x + dx) % NX) * NZ + zi) * NC + core
    hit = jnp.any(ids[:, None] == listed[None, :], axis=1) | (buf == 8)
    tiles = jnp.arange(tile_len.shape[0], dtype=jnp.int32)
    return jnp.sum(jnp.where((ids[:, None] == tiles[None, :]) & hit[:, None], tile_len[None, :], 0), axis=1)


def spread_kernel(k, v, out):
    for h in range(KV):
        at = slice(h * HD, (h + 1) * HD)
        out[h, :, :HD] = k[:, at]
        out[h, :, HD:] = v[:, at]


def spread(keys, values):
    return pl.pallas_call(
        spread_kernel,
        out_shape=jax.ShapeDtypeStruct((KV, keys.shape[0], 2 * HD), BF16),
        in_specs=[VM, VM],
        out_specs=VM,
        cost_estimate=LIGHT,
    )(keys, values)


def local(queries, keys, values, tile_len, ancestors):
    rows = queries.shape[0]
    x, z, c = (lax.axis_index(n) for n in ("x", "z", "c"))

    own = lax.all_to_all(spread(keys, values), "t", 0, 0, tiled=True).reshape(TILE, 2 * HD)
    line = lax.all_to_all(jnp.broadcast_to(own, (NZ, TILE, 2 * HD)), "z", 0, 0, tiled=True)

    eff = seen_lengths(tile_len, ancestors[0], x, z, c)
    q = queries.reshape(rows, KV, GROUP * HD).transpose(1, 0, 2)
    q, eff, line = barrier((q, eff, line))
    q = lax.all_to_all(q, "t", 0, 0, tiled=True).reshape(TILE, GROUP * HD)

    p1 = along(line, 1, FIRST)
    p2 = along(line, -1, NEXT)
    c0 = flip(line)
    state = first(0, eff, q, own, line, c0)
    p3 = along(p1, 1, THIRD)
    c1 = flip_from(p1, 1)
    state = middle(16, eff, q, p1, c1, state)
    c2 = flip_from(p2, 1)
    c3 = flip_from(p3, 2)
    state = middle(32, eff, q, p2, c2, state)
    out = last(48, eff, q, p3, c3, state)

    out = lax.all_to_all(out.reshape(NT, rows, GROUP * HD), "t", 0, 0, tiled=True)
    return out.transpose(1, 0, 2).reshape(rows, HEADS * HD)


def solution(mesh):
    fine = Mesh(mesh.devices.reshape(NX, NZ, NC, NT), ("x", "z", "c", "t"))
    split = P(("x", "z", "c", "t"), None)
    in_specs = (split, split, split, P(), P(("x", "z", "c"), None))
    return jax.shard_map(local, mesh=fine, in_specs=in_specs, out_specs=split, check_vma=False)
```

```python
import functools
import math

import jax
import jax.numpy as jnp
from jax import lax
from jax.experimental import pallas as pl
from jax.experimental.pallas import tpu as pltpu
from jax.sharding import Mesh, PartitionSpec as P

HEADS = 96
KV = 8
HD = 128
TILE = 128
GROUP = HEADS // KV
NX, NZ, NC, NT = 4, 8, 2, 8
BIG = -1e30
OWN = 64
STEP = 16
WIDE = 1024
LOG2E = 1.4426950408889634
SCALE2 = LOG2E / math.sqrt(HD)
F32 = jnp.float32
BF16 = jnp.bfloat16


def soften(s, old):
    parts = [s[:, j : j + HD] for j in range(0, s.shape[1], HD)]
    top = functools.reduce(jnp.maximum, parts)
    new = jnp.maximum(old, jnp.max(top, axis=1, keepdims=True))
    p = jnp.concatenate([jnp.exp2((x - new) * SCALE2).astype(BF16) for x in parts], axis=1)
    return p, jnp.exp2((old - new) * SCALE2), new


def own_tile(own_len, q_ref, own_ref, m_ref, acc_ref):
    row = lax.broadcasted_iota(jnp.int32, (TILE, TILE), 0)
    col = lax.broadcasted_iota(jnp.int32, (TILE, TILE), 1)
    seen = (col <= row) & (col < own_len)
    key_t = own_ref[:, :HD].T
    vext = jnp.concatenate([own_ref[:, HD:], jnp.ones((TILE, HD), BF16)], axis=1)
    for h in range(GROUP):
        s = jnp.dot(q_ref[:, h * HD : (h + 1) * HD], key_t, preferred_element_type=F32)
        s = jnp.where(seen, s, BIG)
        top = jnp.broadcast_to(jnp.max(s, axis=1, keepdims=True), (TILE, HD))
        p = jnp.exp2((s - top) * SCALE2).astype(BF16)
        acc_ref[h] = jnp.dot(p, vext, preferred_element_type=F32)
        m_ref[h] = top


def far_tiles(eff_ref, q_ref, copies, kv_refs, packed, bias, m_ref, acc_ref):
    row = lax.broadcasted_iota(jnp.int32, (TILE, HD), 0)
    lane = lax.broadcasted_iota(jnp.int32, (TILE, HD), 1)
    one = jnp.where(lane == 0, 1.0, 0.0).astype(BF16)
    count = jnp.int32(0)
    slot = 0
    for copy, kv_ref in zip(copies, kv_refs):
        copy.wait()
        for i in range(kv_ref.shape[0]):
            valid = eff_ref[slot]
            at = pl.ds(pl.multiple_of(count, STEP), TILE)
            packed[at, :] = kv_ref[i]
            bias[at, :] = jnp.where(row < valid, 0.0, BIG).astype(BF16)
            count = count + lax.div(valid + (STEP - 1), STEP) * STEP
            slot += 1
    at = pl.ds(pl.multiple_of(count, STEP), WIDE)
    packed[at, :] = jnp.zeros((WIDE, 2 * HD), BF16)
    bias[at, :] = jnp.full((WIDE, HD), BIG, BF16)

    def block(start, size):
        at = pl.ds(pl.multiple_of(start, WIDE // 4), size)
        key_t = jnp.concatenate([packed[at, :HD].T, bias[at, :].T], axis=0)
        vext = jnp.concatenate([packed[at, HD:], jnp.ones((size, HD), BF16)], axis=1)
        for h in range(GROUP):
            q = jnp.concatenate([q_ref[:, h * HD : (h + 1) * HD], one], axis=1)
            s = jnp.dot(q, key_t, preferred_element_type=F32)
            p, keep, m_ref[h] = soften(s, m_ref[h])
            part = jnp.dot(p, vext, preferred_element_type=F32)
            acc_ref[h] = acc_ref[h] * jnp.concatenate([keep, keep], axis=1) + part

    def step(k, carry):
        block(k * WIDE, WIDE)
        return carry

    wide = lax.div(count + (WIDE // 4 - 1), WIDE)
    lax.fori_loop(0, wide, step, 0)
    done = wide * WIDE
    rest = count - done
    half = rest > WIDE // 4

    @pl.when(half)
    def _():
        block(done, WIDE // 2)

    @pl.when((rest > WIDE // 2) | ((rest > 0) & jnp.logical_not(half)))
    def _():
        block(done + jnp.where(half, WIDE // 2, 0), WIDE // 4)


def attend_kernel(eff, q, own, *refs):
    *kv, out, here, m, acc, packed, bias, sems = refs
    here = [here.at[i] for i in range(len(kv))]
    copies = [pltpu.make_async_copy(a, b, sems.at[i]) for i, (a, b) in enumerate(zip(kv, here))]
    for copy in copies:
        copy.start()
    own_tile(eff[OWN], q, own, m, acc)
    far_tiles(eff, q, copies, here, packed, bias, m, acc)
    for h in range(GROUP):
        val = acc[h]
        out[:, h * HD : (h + 1) * HD] = (val[:, :HD] / val[:, HD:]).astype(BF16)


VM = pl.BlockSpec(memory_space=pltpu.VMEM)
SM = pl.BlockSpec(memory_space=pltpu.SMEM)
PARAMS = pltpu.CompilerParams(vmem_limit_bytes=22 * 1024 * 1024)


def busy(us):
    return pl.CostEstimate(flops=int(us * 1e9), bytes_accessed=1024, transcendentals=1024)


LIGHT = pl.CostEstimate(flops=1, bytes_accessed=1, transcendentals=1)


def attend(eff, q, own, *kv):
    rows = len(kv) * NZ * TILE + WIDE
    return pl.pallas_call(
        attend_kernel,
        out_shape=jax.ShapeDtypeStruct((TILE, GROUP * HD), BF16),
        in_specs=[SM, VM, VM] + [pl.BlockSpec(memory_space=pl.ANY)] * len(kv),
        out_specs=VM,
        scratch_shapes=[
            pltpu.VMEM((len(kv), NZ, TILE, 2 * HD), BF16),
            pltpu.VMEM((GROUP, TILE, HD), F32),
            pltpu.VMEM((GROUP, TILE, 2 * HD), F32),
            pltpu.VMEM((rows, 2 * HD), BF16),
            pltpu.VMEM((rows, HD), BF16),
            pltpu.SemaphoreType.DMA((len(kv),)),
        ],
        compiler_params=PARAMS,
        cost_estimate=busy(10),
    )(eff, q, own, *kv)


def flip(a):
    return lax.ppermute(a, "c", [(0, 1), (1, 0)])


def along(a, step, wanted):
    pairs = []
    for x in range(NX):
        for c in range(NC):
            to = (x + step) % NX if c == 0 else (x - step) % NX
            if (c, x, to) in wanted:
                pairs.append((x * NC + c, to * NC + c))
    return lax.ppermute(a, ("x", "c"), pairs)


def flip_from(a, low):
    pairs = [(x * NC + c, x * NC + 1 - c) for x in range(low, NX) for c in range(NC)]
    return lax.ppermute(a, ("x", "c"), pairs)


NEXT = {(c, x, x + 1) for c in range(NC) for x in range(NX - 1)} | {(c, 0, NX - 1) for c in range(NC)}
FIRST = NEXT | {(1, 1, 0)}
THIRD = {(0, 1, 2), (0, 2, 3), (1, 3, 2), (1, 0, 3)}


barrier = lax.optimization_barrier


def seen_lengths(tile_len, listed, x, z, c):
    i = jnp.arange(72, dtype=jnp.int32)
    buf, slot = i // 8, i % 8
    core = jnp.where(buf % 2 == 0, c, 1 - c)
    side = jnp.where(c == 0, -1, 1)
    dx = jnp.where((buf < 2) | (buf == 8), 0, jnp.where(buf >= 6, 2, jnp.where((buf == 2) | (buf == 5), side, -side)))
    zi = jnp.where(buf == 8, z, slot)
    ids = (((x + dx) % NX) * NZ + zi) * NC + core
    hit = jnp.any(ids[:, None] == listed[None, :], axis=1) | (buf == 8)
    tiles = jnp.arange(tile_len.shape[0], dtype=jnp.int32)
    return jnp.sum(jnp.where((ids[:, None] == tiles[None, :]) & hit[:, None], tile_len[None, :], 0), axis=1)


def spread_kernel(k, v, out):
    for h in range(KV):
        at = slice(h * HD, (h + 1) * HD)
        out[h, :, :HD] = k[:, at]
        out[h, :, HD:] = v[:, at]


def spread(keys, values):
    return pl.pallas_call(
        spread_kernel,
        out_shape=jax.ShapeDtypeStruct((KV, keys.shape[0], 2 * HD), BF16),
        in_specs=[VM, VM],
        out_specs=VM,
        cost_estimate=LIGHT,
    )(keys, values)


def local(queries, keys, values, tile_len, ancestors):
    rows = queries.shape[0]
    x, z, c = (lax.axis_index(n) for n in ("x", "z", "c"))

    own = lax.all_to_all(spread(keys, values), "t", 0, 0, tiled=True).reshape(TILE, 2 * HD)
    line = lax.all_to_all(jnp.broadcast_to(own, (NZ, TILE, 2 * HD)), "z", 0, 0, tiled=True)

    eff = seen_lengths(tile_len, ancestors[0], x, z, c)

    p1 = along(line, 1, FIRST)
    p2 = along(line, -1, NEXT)
    c0 = flip(line)
    q = queries.reshape(rows, KV, GROUP * HD).transpose(1, 0, 2)
    q, eff, c0 = barrier((q, eff, c0))
    q = lax.all_to_all(q, "t", 0, 0, tiled=True).reshape(TILE, GROUP * HD)
    p3 = along(p1, 1, THIRD)
    c1 = flip_from(p1, 1)
    c2 = flip_from(p2, 1)
    c3 = flip_from(p3, 2)
    out = attend(eff, q, own, line, c0, p1, c1, p2, c2, p3, c3)

    out = lax.all_to_all(out.reshape(NT, rows, GROUP * HD), "t", 0, 0, tiled=True)
    return out.transpose(1, 0, 2).reshape(rows, HEADS * HD)


def solution(mesh):
    fine = Mesh(mesh.devices.reshape(NX, NZ, NC, NT), ("x", "z", "c", "t"))
    split = P(("x", "z", "c", "t"), None)
    in_specs = (split, split, split, P(), P(("x", "z", "c"), None))
    return jax.shard_map(local, mesh=fine, in_specs=in_specs, out_specs=split, check_vma=False)
```

```python
import functools
import math

import jax
import jax.numpy as jnp
from jax import lax
from jax.experimental import pallas as pl
from jax.experimental.pallas import tpu as pltpu
from jax.sharding import Mesh, PartitionSpec as P

HEADS = 96
KV = 8
HD = 128
TILE = 128
GROUP = HEADS // KV
NX, NZ, NC, NT = 4, 8, 2, 8
BIG = -1e30
OWN = 64
STEP = 16
WIDE = 1024
LOG2E = 1.4426950408889634
SCALE2 = LOG2E / math.sqrt(HD)
F32 = jnp.float32
BF16 = jnp.bfloat16


def soften(s, old):
    parts = [s[:, j : j + HD] for j in range(0, s.shape[1], HD)]
    top = functools.reduce(jnp.maximum, parts)
    new = jnp.maximum(old, jnp.max(top, axis=1, keepdims=True))
    p = jnp.concatenate([jnp.exp2((x - new) * SCALE2).astype(BF16) for x in parts], axis=1)
    return p, jnp.exp2((old - new) * SCALE2), new


def own_tile(own_len, q_ref, own_ref, m_ref, acc_ref):
    row = lax.broadcasted_iota(jnp.int32, (TILE, TILE), 0)
    col = lax.broadcasted_iota(jnp.int32, (TILE, TILE), 1)
    seen = (col <= row) & (col < own_len)
    key_t = own_ref[:, :HD].T
    vext = jnp.concatenate([own_ref[:, HD:], jnp.ones((TILE, HD), BF16)], axis=1)
    for h in range(GROUP):
        s = jnp.dot(q_ref[:, h * HD : (h + 1) * HD], key_t, preferred_element_type=F32)
        s = jnp.where(seen, s, BIG)
        top = jnp.broadcast_to(jnp.max(s, axis=1, keepdims=True), (TILE, HD))
        p = jnp.exp2((s - top) * SCALE2).astype(BF16)
        acc_ref[h] = jnp.dot(p, vext, preferred_element_type=F32)
        m_ref[h] = top


def far_tiles(eff_ref, q_ref, copies, kv_refs, packed, bias, m_ref, acc_ref):
    row = lax.broadcasted_iota(jnp.int32, (TILE, HD), 0)
    lane = lax.broadcasted_iota(jnp.int32, (TILE, HD), 1)
    one = jnp.where(lane == 0, 1.0, 0.0).astype(BF16)
    count = jnp.int32(0)
    slot = 0
    for copy, kv_ref in zip(copies, kv_refs):
        copy.wait()
        for i in range(kv_ref.shape[0]):
            valid = eff_ref[slot]
            at = pl.ds(pl.multiple_of(count, STEP), TILE)
            packed[at, :] = kv_ref[i]
            bias[at, :] = jnp.where(row < valid, 0.0, BIG).astype(BF16)
            count = count + lax.div(valid + (STEP - 1), STEP) * STEP
            slot += 1
    at = pl.ds(pl.multiple_of(count, STEP), WIDE)
    packed[at, :] = jnp.zeros((WIDE, 2 * HD), BF16)
    bias[at, :] = jnp.full((WIDE, HD), BIG, BF16)

    def block(start, size):
        at = pl.ds(pl.multiple_of(start, WIDE // 4), size)
        key_t = jnp.concatenate([packed[at, :HD].T, bias[at, :].T], axis=0)
        vext = jnp.concatenate([packed[at, HD:], jnp.ones((size, HD), BF16)], axis=1)
        for h in range(GROUP):
            q = jnp.concatenate([q_ref[:, h * HD : (h + 1) * HD], one], axis=1)
            s = jnp.dot(q, key_t, preferred_element_type=F32)
            p, keep, m_ref[h] = soften(s, m_ref[h])
            part = jnp.dot(p, vext, preferred_element_type=F32)
            acc_ref[h] = acc_ref[h] * jnp.concatenate([keep, keep], axis=1) + part

    def step(k, carry):
        block(k * WIDE, WIDE)
        return carry

    wide = lax.div(count + (WIDE // 4 - 1), WIDE)
    lax.fori_loop(0, wide, step, 0)
    done = wide * WIDE
    rest = count - done
    half = rest > WIDE // 4

    @pl.when(half)
    def _():
        block(done, WIDE // 2)

    @pl.when((rest > WIDE // 2) | ((rest > 0) & jnp.logical_not(half)))
    def _():
        block(done + jnp.where(half, WIDE // 2, 0), WIDE // 4)


def attend_kernel(eff, q, own, *refs):
    *kv, out, here, m, acc, packed, bias, sems = refs
    here = [here.at[i] for i in range(len(kv))]
    copies = [pltpu.make_async_copy(a, b, sems.at[i]) for i, (a, b) in enumerate(zip(kv, here))]
    for copy in copies:
        copy.start()
    own_tile(eff[OWN], q, own, m, acc)
    far_tiles(eff, q, copies, here, packed, bias, m, acc)
    for h in range(GROUP):
        val = acc[h]
        out[:, h * HD : (h + 1) * HD] = (val[:, :HD] / val[:, HD:]).astype(BF16)


VM = pl.BlockSpec(memory_space=pltpu.VMEM)
SM = pl.BlockSpec(memory_space=pltpu.SMEM)
PARAMS = pltpu.CompilerParams(vmem_limit_bytes=50 * 1024 * 1024)


def busy(us):
    return pl.CostEstimate(flops=int(us * 1e9), bytes_accessed=1024, transcendentals=1024)


LIGHT = pl.CostEstimate(flops=1, bytes_accessed=1, transcendentals=1)


def attend(eff, q, own, *kv):
    rows = len(kv) * NZ * TILE + WIDE
    return pl.pallas_call(
        attend_kernel,
        out_shape=jax.ShapeDtypeStruct((TILE, GROUP * HD), BF16),
        in_specs=[SM, VM, VM] + [pl.BlockSpec(memory_space=pl.ANY)] * len(kv),
        out_specs=VM,
        scratch_shapes=[
            pltpu.VMEM((len(kv), NZ, TILE, 2 * HD), BF16),
            pltpu.VMEM((GROUP, TILE, HD), F32),
            pltpu.VMEM((GROUP, TILE, 2 * HD), F32),
            pltpu.VMEM((rows, 2 * HD), BF16),
            pltpu.VMEM((rows, HD), BF16),
            pltpu.SemaphoreType.DMA((len(kv),)),
        ],
        compiler_params=PARAMS,
        cost_estimate=busy(10),
    )(eff, q, own, *kv)


def flip(a):
    return lax.ppermute(a, "c", [(0, 1), (1, 0)])


def along(a, step, wanted):
    pairs = []
    for x in range(NX):
        for c in range(NC):
            to = (x + step) % NX if c == 0 else (x - step) % NX
            if (c, x, to) in wanted:
                pairs.append((x * NC + c, to * NC + c))
    return lax.ppermute(a, ("x", "c"), pairs)


def flip_from(a, low):
    pairs = [(x * NC + c, x * NC + 1 - c) for x in range(low, NX) for c in range(NC)]
    return lax.ppermute(a, ("x", "c"), pairs)


NEXT = {(c, x, x + 1) for c in range(NC) for x in range(NX - 1)} | {(c, 0, NX - 1) for c in range(NC)}
FIRST = NEXT | {(1, 1, 0)}
THIRD = {(0, 1, 2), (0, 2, 3), (1, 3, 2), (1, 0, 3)}


barrier = lax.optimization_barrier


def seen_lengths(tile_len, listed, x, z, c):
    i = jnp.arange(72, dtype=jnp.int32)
    buf, slot = i // 8, i % 8
    core = jnp.where(buf % 2 == 0, c, 1 - c)
    side = jnp.where(c == 0, -1, 1)
    dx = jnp.where((buf < 2) | (buf == 8), 0, jnp.where(buf >= 6, 2, jnp.where((buf == 2) | (buf == 5), side, -side)))
    zi = jnp.where(buf == 8, z, slot)
    ids = (((x + dx) % NX) * NZ + zi) * NC + core
    hit = jnp.any(ids[:, None] == listed[None, :], axis=1) | (buf == 8)
    tiles = jnp.arange(tile_len.shape[0], dtype=jnp.int32)
    return jnp.sum(jnp.where((ids[:, None] == tiles[None, :]) & hit[:, None], tile_len[None, :], 0), axis=1)


def spread_kernel(k, v, out):
    for h in range(KV):
        at = slice(h * HD, (h + 1) * HD)
        out[h, :, :HD] = k[:, at]
        out[h, :, HD:] = v[:, at]


def spread(keys, values):
    return pl.pallas_call(
        spread_kernel,
        out_shape=jax.ShapeDtypeStruct((KV, keys.shape[0], 2 * HD), BF16),
        in_specs=[VM, VM],
        out_specs=VM,
        cost_estimate=LIGHT,
    )(keys, values)


def local(queries, keys, values, tile_len, ancestors):
    rows = queries.shape[0]
    x, z, c = (lax.axis_index(n) for n in ("x", "z", "c"))

    own = lax.all_to_all(spread(keys, values), "t", 0, 0, tiled=True).reshape(TILE, 2 * HD)
    line = lax.all_to_all(jnp.broadcast_to(own, (NZ, TILE, 2 * HD)), "z", 0, 0, tiled=True)

    eff = seen_lengths(tile_len, ancestors[0], x, z, c)

    p1 = along(line, 1, FIRST)
    p2 = along(line, -1, NEXT)
    c0 = flip(line)
    q = queries.reshape(rows, KV, GROUP * HD).transpose(1, 0, 2)
    q, eff, c0 = barrier((q, eff, c0))
    q = lax.all_to_all(q, "t", 0, 0, tiled=True).reshape(TILE, GROUP * HD)
    p3 = along(p1, 1, THIRD)
    c1 = flip_from(p1, 1)
    c2 = flip_from(p2, 1)
    c3 = flip_from(p3, 2)
    out = attend(eff, q, own, line, c0, p1, c1, p2, c2, p3, c3)

    out = lax.all_to_all(out.reshape(NT, rows, GROUP * HD), "t", 0, 0, tiled=True)
    return out.transpose(1, 0, 2).reshape(rows, HEADS * HD)


def solution(mesh):
    fine = Mesh(mesh.devices.reshape(NX, NZ, NC, NT), ("x", "z", "c", "t"))
    split = P(("x", "z", "c", "t"), None)
    in_specs = (split, split, split, P(), P(("x", "z", "c"), None))
    return jax.shard_map(local, mesh=fine, in_specs=in_specs, out_specs=split, check_vma=False)
```

```python
import functools
import math

import jax
import jax.numpy as jnp
from jax import lax
from jax.experimental import pallas as pl
from jax.experimental.pallas import tpu as pltpu
from jax.sharding import Mesh, PartitionSpec as P

HEADS = 96
KV = 8
HD = 128
TILE = 128
GROUP = HEADS // KV
NX, NZ, NC, NT = 4, 8, 2, 8
BIG = -1e30
OWN = 64
STEP = 16
WIDE = 1024
LOG2E = 1.4426950408889634
SCALE2 = LOG2E / math.sqrt(HD)
F32 = jnp.float32
BF16 = jnp.bfloat16


def soften(s, old):
    parts = [s[:, j : j + HD] for j in range(0, s.shape[1], HD)]
    top = functools.reduce(jnp.maximum, parts)
    new = jnp.maximum(old, jnp.max(top, axis=1, keepdims=True))
    p = jnp.concatenate([jnp.exp2((x - new) * SCALE2).astype(BF16) for x in parts], axis=1)
    return p, jnp.exp2((old - new) * SCALE2), new


def own_tile(own_len, q_ref, own_ref, m_ref, acc_ref):
    row = lax.broadcasted_iota(jnp.int32, (TILE, TILE), 0)
    col = lax.broadcasted_iota(jnp.int32, (TILE, TILE), 1)
    seen = (col <= row) & (col < own_len)
    key_t = own_ref[:, :HD].T
    vext = jnp.concatenate([own_ref[:, HD:], jnp.ones((TILE, HD), BF16)], axis=1)
    for h in range(GROUP):
        s = jnp.dot(q_ref[:, h * HD : (h + 1) * HD], key_t, preferred_element_type=F32)
        s = jnp.where(seen, s, BIG)
        top = jnp.broadcast_to(jnp.max(s, axis=1, keepdims=True), (TILE, HD))
        p = jnp.exp2((s - top) * SCALE2).astype(BF16)
        acc_ref[h] = jnp.dot(p, vext, preferred_element_type=F32)
        m_ref[h] = top


def far_tiles(eff_ref, base, q_ref, kv_refs, packed, bias, m_ref, acc_ref):
    row = lax.broadcasted_iota(jnp.int32, (TILE, HD), 0)
    lane = lax.broadcasted_iota(jnp.int32, (TILE, HD), 1)
    one = jnp.where(lane == 0, 1.0, 0.0).astype(BF16)
    count = jnp.int32(0)
    slot = base
    for kv_ref in kv_refs:
        for i in range(kv_ref.shape[0]):
            valid = eff_ref[slot]
            at = pl.ds(pl.multiple_of(count, STEP), TILE)
            packed[at, :] = kv_ref[i]
            bias[at, :] = jnp.where(row < valid, 0.0, BIG).astype(BF16)
            count = count + lax.div(valid + (STEP - 1), STEP) * STEP
            slot += 1
    at = pl.ds(pl.multiple_of(count, STEP), WIDE)
    packed[at, :] = jnp.zeros((WIDE, 2 * HD), BF16)
    bias[at, :] = jnp.full((WIDE, HD), BIG, BF16)

    def block(start, size):
        at = pl.ds(pl.multiple_of(start, WIDE // 4), size)
        key_t = jnp.concatenate([packed[at, :HD].T, bias[at, :].T], axis=0)
        vext = jnp.concatenate([packed[at, HD:], jnp.ones((size, HD), BF16)], axis=1)
        for h in range(GROUP):
            q = jnp.concatenate([q_ref[:, h * HD : (h + 1) * HD], one], axis=1)
            s = jnp.dot(q, key_t, preferred_element_type=F32)
            p, keep, m_ref[h] = soften(s, m_ref[h])
            part = jnp.dot(p, vext, preferred_element_type=F32)
            acc_ref[h] = acc_ref[h] * jnp.concatenate([keep, keep], axis=1) + part

    def step(k, carry):
        block(k * WIDE, WIDE)
        return carry

    wide = lax.div(count + (WIDE // 4 - 1), WIDE)
    lax.fori_loop(0, wide, step, 0)
    done = wide * WIDE
    rest = count - done
    half = rest > WIDE // 4

    @pl.when(half)
    def _():
        block(done, WIDE // 2)

    @pl.when((rest > WIDE // 2) | ((rest > 0) & jnp.logical_not(half)))
    def _():
        block(done + jnp.where(half, WIDE // 2, 0), WIDE // 4)


def first_kernel(base, eff, q, own, *refs):
    *kv, m, acc, packed, bias = refs
    own_tile(eff[OWN], q, own, m, acc)
    far_tiles(eff, base, q, kv, packed, bias, m, acc)


def last_kernel(base, eff, q, m_in, acc_in, *refs):
    *kv, out, m, acc, packed, bias = refs
    m[...] = m_in[...]
    acc[...] = acc_in[...]
    far_tiles(eff, base, q, kv, packed, bias, m, acc)
    for h in range(GROUP):
        val = acc[h]
        out[:, h * HD : (h + 1) * HD] = (val[:, :HD] / val[:, HD:]).astype(BF16)


VM = pl.BlockSpec(memory_space=pltpu.VMEM)
SM = pl.BlockSpec(memory_space=pltpu.SMEM)
STATE = (
    jax.ShapeDtypeStruct((GROUP, TILE, HD), F32),
    jax.ShapeDtypeStruct((GROUP, TILE, 2 * HD), F32),
)


def work(kv):
    rows = sum(a.shape[0] for a in kv) * TILE + WIDE
    return [pltpu.VMEM((rows, 2 * HD), BF16), pltpu.VMEM((rows, HD), BF16)]


PARAMS = pltpu.CompilerParams(vmem_limit_bytes=24 * 1024 * 1024)


def busy(us):
    return pl.CostEstimate(flops=int(us * 1e9), bytes_accessed=1024, transcendentals=1024)


LIGHT = pl.CostEstimate(flops=1, bytes_accessed=1, transcendentals=1)


def first(base, eff, q, own, *kv):
    return pl.pallas_call(
        functools.partial(first_kernel, base),
        out_shape=STATE,
        in_specs=[SM, VM, VM] + [VM] * len(kv),
        out_specs=(VM, VM),
        scratch_shapes=work(kv),
        compiler_params=PARAMS,
        cost_estimate=busy(6),
    )(eff, q, own, *kv)


def last(base, eff, q, state, *kv):
    return pl.pallas_call(
        functools.partial(last_kernel, base),
        out_shape=jax.ShapeDtypeStruct((TILE, GROUP * HD), BF16),
        in_specs=[SM, VM, VM, VM] + [VM] * len(kv),
        out_specs=VM,
        scratch_shapes=[pltpu.VMEM(s.shape, s.dtype) for s in STATE] + work(kv),
        compiler_params=PARAMS,
        cost_estimate=busy(4),
    )(eff, q, *state, *kv)


def flip(a):
    return lax.ppermute(a, "c", [(0, 1), (1, 0)])


def along(a, step, wanted):
    pairs = []
    for x in range(NX):
        for c in range(NC):
            to = (x + step) % NX if c == 0 else (x - step) % NX
            if (c, x, to) in wanted:
                pairs.append((x * NC + c, to * NC + c))
    return lax.ppermute(a, ("x", "c"), pairs)


def flip_from(a, low):
    pairs = [(x * NC + c, x * NC + 1 - c) for x in range(low, NX) for c in range(NC)]
    return lax.ppermute(a, ("x", "c"), pairs)


NEXT = {(c, x, x + 1) for c in range(NC) for x in range(NX - 1)} | {(c, 0, NX - 1) for c in range(NC)}
FIRST = NEXT | {(1, 1, 0)}
THIRD = {(0, 1, 2), (0, 2, 3), (1, 3, 2), (1, 0, 3)}


barrier = lax.optimization_barrier


def seen_lengths(tile_len, listed, x, z, c):
    i = jnp.arange(72, dtype=jnp.int32)
    buf, slot = i // 8, i % 8
    core = jnp.where(buf % 2 == 0, c, 1 - c)
    side = jnp.where(c == 0, -1, 1)
    dx = jnp.where((buf < 2) | (buf == 8), 0, jnp.where(buf >= 6, 2, jnp.where((buf == 2) | (buf == 5), side, -side)))
    zi = jnp.where(buf == 8, z, slot)
    ids = (((x + dx) % NX) * NZ + zi) * NC + core
    hit = jnp.any(ids[:, None] == listed[None, :], axis=1) | (buf == 8)
    tiles = jnp.arange(tile_len.shape[0], dtype=jnp.int32)
    return jnp.sum(jnp.where((ids[:, None] == tiles[None, :]) & hit[:, None], tile_len[None, :], 0), axis=1)


def spread_kernel(k, v, out):
    for h in range(KV):
        at = slice(h * HD, (h + 1) * HD)
        out[h, :, :HD] = k[:, at]
        out[h, :, HD:] = v[:, at]


def spread(keys, values):
    return pl.pallas_call(
        spread_kernel,
        out_shape=jax.ShapeDtypeStruct((KV, keys.shape[0], 2 * HD), BF16),
        in_specs=[VM, VM],
        out_specs=VM,
        cost_estimate=LIGHT,
    )(keys, values)


def local(queries, keys, values, tile_len, ancestors):
    rows = queries.shape[0]
    x, z, c = (lax.axis_index(n) for n in ("x", "z", "c"))

    own = lax.all_to_all(spread(keys, values), "t", 0, 0, tiled=True).reshape(TILE, 2 * HD)
    line = lax.all_to_all(jnp.broadcast_to(own, (NZ, TILE, 2 * HD)), "z", 0, 0, tiled=True)

    eff = seen_lengths(tile_len, ancestors[0], x, z, c)

    p1 = along(line, 1, FIRST)
    p2 = along(line, -1, NEXT)
    c0 = flip(line)
    q = queries.reshape(rows, KV, GROUP * HD).transpose(1, 0, 2)
    q, eff, c0 = barrier((q, eff, c0))
    q = lax.all_to_all(q, "t", 0, 0, tiled=True).reshape(TILE, GROUP * HD)
    p3 = along(p1, 1, THIRD)
    c1 = flip_from(p1, 1)
    c2 = flip_from(p2, 1)
    c3 = flip_from(p3, 2)
    state = first(0, eff, q, own, line, c0, p1, c1, p2, c2)
    out = last(48, eff, q, state, p3, c3)

    out = lax.all_to_all(out.reshape(NT, rows, GROUP * HD), "t", 0, 0, tiled=True)
    return out.transpose(1, 0, 2).reshape(rows, HEADS * HD)


def solution(mesh):
    fine = Mesh(mesh.devices.reshape(NX, NZ, NC, NT), ("x", "z", "c", "t"))
    split = P(("x", "z", "c", "t"), None)
    in_specs = (split, split, split, P(), P(("x", "z", "c"), None))
    return jax.shard_map(local, mesh=fine, in_specs=in_specs, out_specs=split, check_vma=False)
```
